32 devices in a mesh: rows: 16 (over z, y, x), seq: 2 (over core).
Axes of the slice: x: 2, y: 2, z: 4, core: 2. Of those that a mesh axis runs over, the one named last changes fastest.
Arguments:
- tokens: bfloat16 [16, 1024, 768], P('rows', 'seq'), may hold values from -8 to 8
- segment_ids: int32 [16, 1024], P('rows'), may hold values from -1 to 4, as said below
- ln1_gain: bfloat16 [768], replicated, may hold values from 0.099609375 to 1.8984375
- ln1_bias: bfloat16 [768], replicated, may hold values from -2 to 2
- w_qkv: bfloat16 [768, 2304], replicated, may hold values from -0.21875 to 0.21875
- bias_q: bfloat16 [768], replicated, may hold values from -2 to 2
- bias_v: bfloat16 [768], replicated, may hold values from -3 to 3
- w_proj: bfloat16 [768, 768], replicated, may hold values from -0.875 to 0.875
- bias_proj: bfloat16 [768], replicated, may hold values from -2 to 2
- ln2_gain: bfloat16 [768], replicated, may hold values from 0.099609375 to 1.8984375
- ln2_bias: bfloat16 [768], replicated, may hold values from -2 to 2
- w_fc1: bfloat16 [768, 3072], replicated, may hold values from -0.21875 to 0.21875
- bias_fc1: bfloat16 [3072], replicated, may hold values from -3 to 3
- w_fc2: bfloat16 [3072, 768], replicated, may hold values from -0.109375 to 0.109375
- bias_fc2: bfloat16 [768], replicated, may hold values from -2 to 2
- cotangent: bfloat16 [16, 1024, 768], P('rows', 'seq'), may hold values from -6 to 6
Outputs:
- output: bfloat16 [16, 1024, 768], P('rows', 'seq')
- grad_tokens: float32 [16, 1024, 768], P('rows', 'seq')
- grad_ln1_gain: float32 [768], replicated
- grad_ln1_bias: float32 [768], replicated
- grad_w_qkv: float32 [1769472], P('rows')
- grad_bias_q: float32 [768], replicated
- grad_bias_v: float32 [768], replicated
- grad_w_proj: float32 [589824], P('rows')
- grad_bias_proj: float32 [768], replicated
- grad_ln2_gain: float32 [768], replicated
- grad_ln2_bias: float32 [768], replicated
- grad_w_fc1: float32 [2359296], P('rows')
- grad_bias_fc1: float32 [3072], replicated
- grad_w_fc2: float32 [2359296], P('rows')
- grad_bias_fc2: float32 [768], replicated
- variance: float32 [768], replicated
The draws below stay inside these ranges and needn't reach their ends.
Inputs may be any that keep to these rules, and one draw needn't show every extreme that they name: `segment_ids`: along each row the ids never fall until padding; -1 marks padding, which only ends a row and takes one position or more; every row holds the images 0 to 4. Each image holds at most 256 positions; in every row the image that holds positions 511 and 512 holds exactly 256.
All inputs are finite; a program needn't handle non-finite values.
Results may differ from the reference program's by a relative error of at most 0.012.
Values may be sent and summed in bfloat16 or wider, within the bound.
No kernel may reach another device: no remote copies, remote signals or barrier semaphores. Data moves between devices by JAX's collectives and lax.ppermute only.
A program may use at most 192 MiB of HBM per device.

```python
import jax
import jax.numpy as jnp
from jax import lax

D = 768
HEADS = 12
HEAD_DIM = 64
FF = 3072
ROW_LEN = 1024
ROWS = 16
IMAGE_MOST = 256


def draw_tokens(key, part):
    key = jax.random.fold_in(key, 2)
    first_key = jax.random.fold_in(key, 0)
    ramp = 0.5 + jnp.arange(ROWS, dtype=jnp.float32) / (ROWS - 1)
    value = jax.random.normal(first_key, (ROWS, ROW_LEN, D), jnp.float32) * ramp[:, None, None]
    return jnp.clip(value, -8.0, 8.0).astype(jnp.bfloat16)


def draw_segment_ids(key, part):
    key = jax.random.fold_in(key, 5)
    first_key, second_key, third_key, fourth_key = jax.random.split(key, 4)
    jitter = max(1, ROW_LEN // 128)
    before = jax.random.randint(first_key, (ROWS, 1), IMAGE_MOST // 4, 3 * IMAGE_MOST // 4 + 1, jnp.int32)
    middle_start = ROW_LEN // 2 - before
    middle_end = middle_start + IMAGE_MOST
    padding = jax.random.randint(second_key, (ROWS, 1), 1, ROW_LEN // 16 + 1, jnp.int32)
    row_end = ROW_LEN - padding
    first_cut = middle_start // 2 + jax.random.randint(third_key, (ROWS, 1), -jitter, jitter + 1, jnp.int32)
    last_cut = (middle_end + row_end) // 2 + jax.random.randint(fourth_key, (ROWS, 1), -jitter, jitter + 1, jnp.int32)
    bounds = jnp.concatenate([first_cut, middle_start, middle_end, last_cut], 1)
    places = jnp.arange(ROW_LEN, dtype=jnp.int32)
    images = jnp.sum((places[None, :, None] >= bounds[:, None, :]).astype(jnp.int32), -1)
    return jnp.where(places[None, :] >= row_end, -1, images).astype(jnp.int32)


def block_levels(key, extent, pieces, low, high):
    loudness, own = 1.0, jax.random.fold_in(key, 6)
    for axis_at, shards_of in pieces:
        steps = jnp.exp(jax.random.uniform(jax.random.fold_in(own, axis_at), (shards_of,), jnp.float32, low / len(pieces), high / len(pieces)))
        loudness = loudness * jnp.repeat(steps, extent[axis_at] // shards_of).reshape([-1 if axis == axis_at else 1 for axis in range(len(extent))])
    return loudness


def bell_draw(stream_key, shape, scale, most, cuts=(), kind=jnp.bfloat16):
    factor_of = block_levels(stream_key, shape, cuts, -0.22, 0.18) if cuts else 1.0
    drawn = jax.random.normal(stream_key, shape, jnp.float32) * scale * factor_of
    return jnp.minimum(jnp.maximum(drawn, -most), most).astype(kind)


def setup_inputs(seed: int = 0) -> dict:
    key_list = jax.random.split(jax.random.key(seed), 17)
    return {
        "tokens": draw_tokens(jax.random.fold_in(key_list[16], 71), 0),
        "segment_ids": draw_segment_ids(jax.random.fold_in(key_list[16], 71), 0),
        "ln1_gain": jnp.clip(1.0 + 0.18 * jax.random.normal(key_list[2], (D,), jnp.float32), 0.099609375, 1.8984375).astype(jnp.bfloat16),
        "ln1_bias": bell_draw(key_list[3], (D,), 0.3, 2.0),
        "w_qkv": bell_draw(key_list[4], (D, 3 * D), D ** -0.5, 0.21875),
        "bias_q": bell_draw(key_list[5], (D,), 0.3, 2.0),
        "bias_v": bell_draw(key_list[6], (D,), 0.5, 3.0),
        "w_proj": bell_draw(key_list[7], (D, D), (D // 16) ** -0.5, 0.875),
        "bias_proj": bell_draw(key_list[8], (D,), 0.3, 2.0),
        "ln2_gain": jnp.clip(1.0 + 0.18 * jax.random.normal(key_list[9], (D,), jnp.float32), 0.099609375, 1.8984375).astype(jnp.bfloat16),
        "ln2_bias": bell_draw(key_list[10], (D,), 0.3, 2.0),
        "w_fc1": bell_draw(key_list[11], (D, FF), D ** -0.5, 0.21875),
        "bias_fc1": bell_draw(key_list[12], (FF,), 0.5, 3.0),
        "w_fc2": bell_draw(key_list[13], (FF, D), FF ** -0.5, 0.109375),
        "bias_fc2": bell_draw(key_list[14], (D,), 0.3, 2.0),
        "cotangent": bell_draw(key_list[15], (ROWS, ROW_LEN, D), 1.0, 6.0, ((0, 16), (1, 2))),
    }


norm_epsilon = 1e-06

@jax.custom_vjp
def low(v):
    return lax.optimization_barrier(v.astype(jnp.bfloat16)).astype(jnp.float32)

@jax.custom_vjp
def low_back(v):
    return v

def low_keep(v):
    return (low(v), None)

def low_pass(kept, grad):
    return (grad,)

def back_keep(v):
    return (v, None)

def back_low(kept, grad):
    return (low(grad),)
low.defvjp(low_keep, low_pass)
low_back.defvjp(back_keep, back_low)

def norm_rows(value, gain, shift):
    centre = lax.optimization_barrier(jnp.mean(value, -1, keepdims=True))
    centred = value - centre
    spread = lax.optimization_barrier(jnp.mean(centred * centred, -1, keepdims=True))
    return centred * lax.rsqrt(spread + norm_epsilon) * gain + shift

def forward(inputs, params, segments):
    ln1_gain, ln1_bias, w_qkv, bias_q, bias_v, w_proj, bias_proj, ln2_gain, ln2_bias, w_fc1, bias_fc1, w_fc2, bias_fc2 = params
    row_length, features = inputs.shape
    highest = lax.Precision.HIGHEST
    normed = low(norm_rows(inputs, ln1_gain, ln1_bias))
    mixed = jnp.dot(normed, w_qkv, precision=highest)
    queries = low(low_back(mixed[:, :features] + bias_q))
    key_rows = low(low_back(mixed[:, features:2 * features]))
    value_rows = low(low_back(mixed[:, 2 * features:] + bias_v))
    shaped = (row_length, HEADS, HEAD_DIM)
    scores = jnp.einsum('qhe,khe->hqk', queries.reshape(shaped), key_rows.reshape(shaped), precision=highest) * HEAD_DIM ** (-0.5)
    allowed = (segments[:, None] == segments[None, :]) & (segments[:, None] >= 0)
    scores = low_back(jnp.where(allowed[None], scores, -1e+30))
    row_top = lax.optimization_barrier(jnp.max(scores, -1, keepdims=True))
    exps = jnp.exp(scores - row_top)
    probs = low(exps / lax.optimization_barrier(jnp.sum(exps, -1, keepdims=True)))
    attended = jnp.einsum('hqk,khe->qhe', probs, value_rows.reshape(shaped), precision=highest).reshape(row_length, features)
    valid_rows = (segments >= 0).astype(jnp.float32)[:, None]
    attended = low(low_back(attended * valid_rows))
    branch = low_back(jnp.dot(attended, w_proj, precision=highest) + bias_proj)
    middle = inputs + branch
    normed_two = low(norm_rows(middle, ln2_gain, ln2_bias))
    hidden = low_back(jnp.dot(normed_two, w_fc1, precision=highest) + bias_fc1)
    active_low = low(jax.nn.gelu(hidden, approximate=False))
    branch_two = low_back(jnp.dot(active_low, w_fc2, precision=highest) + bias_fc2)
    return middle + branch_two

def reference(tokens, segment_ids, ln1_gain, ln1_bias, w_qkv, bias_q, bias_v, w_proj, bias_proj, ln2_gain, ln2_bias, w_fc1, bias_fc1, w_fc2, bias_fc2, cotangent):
    params = tuple((weight_arg.astype(jnp.float32) for weight_arg in (ln1_gain, ln1_bias, w_qkv, bias_q, bias_v, w_proj, bias_proj, ln2_gain, ln2_bias, w_fc1, bias_fc1, w_fc2, bias_fc2)))
    zero_grads = tuple((jnp.zeros(weight_arg.shape, jnp.float32) for weight_arg in params))

    def scan_step(state_carry, row_inputs):
        totals, moment_one, moment_two, kept_count = state_carry
        row_tokens, row_segments, row_cotangent = row_inputs

        def run_row(inputs, *weights):
            return forward(inputs, weights, row_segments)
        final, pull_back = jax.vjp(run_row, row_tokens.astype(jnp.float32), *params)
        grad_list = pull_back(row_cotangent.astype(jnp.float32))
        valid_rows = (row_segments >= 0).astype(jnp.float32)[:, None]
        totals = tuple((old + new for old, new in zip(totals, grad_list[1:])))
        moment_one = moment_one + lax.optimization_barrier(jnp.sum(final * valid_rows, 0))
        moment_two = moment_two + lax.optimization_barrier(jnp.sum(final * final * valid_rows, 0))
        kept_count = kept_count + jnp.sum(valid_rows)
        return ((totals, moment_one, moment_two, kept_count), (final.astype(jnp.bfloat16), grad_list[0]))
    start_state = (zero_grads, jnp.zeros((D,), jnp.float32), jnp.zeros((D,), jnp.float32), jnp.zeros((), jnp.float32))
    end_state, stacked = lax.scan(scan_step, start_state, (tokens, segment_ids, cotangent))
    totals, moment_one, moment_two, kept_count = end_state
    output, grad_tokens = stacked
    channel_mean = moment_one / kept_count
    variance = moment_two / kept_count - channel_mean * channel_mean
    return (output, grad_tokens, totals[0], totals[1], totals[2].reshape(-1), totals[3], totals[4], totals[5].reshape(-1), totals[6], totals[7], totals[8], totals[9].reshape(-1), totals[10], totals[11].reshape(-1), totals[12], variance)
```

```python
import functools

import jax
import jax.numpy as jnp
from jax import lax
from jax.experimental import pallas as pl
from jax.experimental.pallas import tpu as pltpu
from jax.sharding import PartitionSpec as P

D = 768
HEAD_DIM = 64
HEADS = 12
FF = 3072
HALO = 256
QUERY_TILE = 128
KEY_TILES = (3, 4, 5, 5)
BIAS_AT = (0, 384, 896, 1536)
BIAS_ROWS = 2176
NORM_EPSILON = 1e-06
F32 = jnp.float32
BF16 = jnp.bfloat16
MIB = 1 << 20
SCALE = 1.15e9
COST = {
    "qkv": 6,
    "attend": 12,
    "mlp": 22,
    "fc2_grad": 7,
    "attend_back": 4,
    "fc1_grad": 5,
    "qkv_grad": 3,
    "input_grad": 4,
    "fold": 2,
    "total": 2,
    "join": 2,
    "results": 2,
    "add": 2,
}


def full(shape):
    return pl.BlockSpec(shape, lambda *_: (0,) * len(shape))


def once(shape):
    return pl.BlockSpec(shape, lambda *_: (0,) * len(shape), pipeline_mode=pl.Buffered(1))


def mm(left, right):
    return lax.dot_general(left, right, (((1,), (0,)), ((), ())), preferred_element_type=F32)


def mm_nt(left, right):
    return lax.dot_general(left, right, (((1,), (1,)), ((), ())), preferred_element_type=F32)


class Stays:
    def __init__(self, value):
        self.value = value


def stays(shape, dtype):
    return pltpu.HBM(shape, dtype)


def moves(shape, dtype):
    return jax.ShapeDtypeStruct(shape, dtype)


def call(kernel, name, grid, in_specs, out_specs, out_shape, args, scratch=(), after=(), vmem=32, cost=None):
    skip = len(after)

    def body(info, *refs):
        kernel(info, *refs[skip:])

    def keep(arg):
        return pltpu.with_memory_space_constraint(arg.value, pltpu.HBM) if isinstance(arg, Stays) else arg

    rest = [keep(arg) for arg in (*after, *args[1:])]
    return pl.pallas_call(
        body if skip else kernel,
        name=name,
        grid_spec=pltpu.PrefetchScalarGridSpec(
            num_scalar_prefetch=1,
            grid=grid,
            in_specs=[pl.BlockSpec(memory_space=pl.ANY)] * skip + list(in_specs),
            out_specs=out_specs,
            scratch_shapes=list(scratch),
        ),
        out_shape=out_shape,
        compiler_params=pltpu.CompilerParams(vmem_limit_bytes=vmem * MIB),
        cost_estimate=pl.CostEstimate(flops=int(SCALE * (cost or COST[name])), bytes_accessed=0, transcendentals=0),
    )(args[0], *rest)


def norm_unit(value):
    centred = value - jnp.mean(value, -1, keepdims=True)
    inv_scale = lax.rsqrt(jnp.mean(centred * centred, -1, keepdims=True) + NORM_EPSILON)
    return centred * inv_scale, inv_scale


def norm_back(grad, unit, inv_scale, gain):
    lifted = grad * gain
    return inv_scale * (
        lifted
        - jnp.mean(lifted, -1, keepdims=True)
        - unit * jnp.mean(lifted * unit, -1, keepdims=True)
    )


def row_of(ref):
    return ref[...].astype(F32).reshape(1, -1)


def begin(copies):
    for copy in copies:
        copy.start()


def finish(copies):
    for copy in copies:
        copy.wait()


def column_valid(seg_ref, core, out_ref):
    for at in range(4):
        row = seg_ref[:, pl.ds(pl.multiple_of(core * 512 + at * 128, 128), 128)]
        valid = jnp.where(row >= 0, 1.0, 0.0).astype(F32)
        out_ref[pl.ds(at * 128, 128), :] = jnp.broadcast_to(valid, (128, 128)).T


def qkv_kernel(info, tok_ref, gain_ref, shift_ref, bq_ref, bv_ref, w_hbm, qkv_ref, normt_ref, low, w, sems):
    step = pl.program_id(0)

    def fetch(n):
        lanes = pl.ds(pl.multiple_of(n * D, D), D)
        return pltpu.make_async_copy(w_hbm.at[:, lanes], w.at[n], sems.at[n])

    @pl.when(step == 0)
    def _():
        begin([fetch(n) for n in range(3)])
        own, _ = norm_unit(tok_ref[...].astype(F32))
        own = (own * row_of(gain_ref) + row_of(shift_ref)).astype(BF16)
        low[...] = own
        normt_ref[...] = own.T

    fetch(step).wait()
    zero = jnp.zeros((1, D), F32)
    shift = jnp.where(step == 0, row_of(bq_ref), jnp.where(step == 1, zero, row_of(bv_ref)))
    scale = jnp.where(step == 0, HEAD_DIM ** (-0.5), 1.0)
    qkv_ref[...] = ((mm(low[...], w[step]) + shift) * scale).astype(BF16)


def qkv_call(info, tok, gain, shift, w, bq, bv):
    return call(
        qkv_kernel,
        "qkv",
        (3,),
        [once((512, D))] + [once((D,))] * 4 + [pl.BlockSpec(memory_space=pl.ANY)],
        [pl.BlockSpec((512, D), lambda n, info: (0, n)), full((D, 512))],
        [stays((512, 3 * D), BF16), moves((D, 512), BF16)],
        (info, Stays(tok), Stays(gain), Stays(shift), Stays(bq), Stays(bv), Stays(w)),
        [pltpu.VMEM((512, D), BF16), pltpu.VMEM((3, D, D), BF16), pltpu.SemaphoreType.DMA((3,))],
    )


def build_bias(seg_ref, core, segk, bias):
    for at in range(6):
        row = seg_ref[:, pl.ds(pl.multiple_of(core * 256 + at * 128, 128), 128)].astype(F32)
        segk[pl.ds(at * 128, 128), :] = jnp.broadcast_to(row, (128, 128)).T
    for i, tiles in enumerate(KEY_TILES):
        width = tiles * 128
        key_at, own_at = tile_place(i, core)
        seg_q = seg_ref[:, pl.ds(pl.multiple_of(core * 512 + own_at, 128), 128)].astype(F32)
        seg_k = segk[pl.ds(pl.multiple_of(key_at, 128), width), :]
        allowed = (seg_k == seg_q) & (seg_q >= 0)
        bias[pl.ds(BIAS_AT[i], width), :] = jnp.where(allowed, 0.0, -1e30)


def tile_place(i, core):
    own_at = jnp.where(core == 0, i, 3 - i) * 128
    key_at = jnp.where(core == 0, (0, 0, 0, 1)[i], (3, 2, 1, 0)[i]) * 128
    return key_at, own_at


def stack_heads(block):
    low = lax.broadcasted_iota(jnp.int32, block.shape, 1) < HEAD_DIM
    zero = jnp.zeros_like(block)
    return jnp.concatenate([jnp.where(low, block, zero), jnp.where(low, zero, block)], 0)


def own_rows(core):
    return pl.ds(pl.multiple_of(core * HALO, HALO), 512)


def halo_rows(core):
    return pl.ds(pl.multiple_of((1 - core) * 512, HALO), HALO)


def attend_kernel(
    info, seg_ref, tok_ref, gain_ref, shift_ref, wk_ref, wv_ref, bv_ref, q_ref, k_ref, v_ref,
    att_ref, attt_ref, lse_ref, hk_ref, hv_ref, segk, bias, halo, shift_v, kx, vx, vt
):
    core = info[0]

    @pl.when(pl.program_id(0) == 0)
    def _():
        build_bias(seg_ref, core, segk, bias)
        unit, _ = norm_unit(tok_ref[...].astype(F32))
        halo[...] = (unit * row_of(gain_ref) + row_of(shift_ref)).astype(BF16)
        shift_v[...] = row_of(bv_ref)

    lanes = pl.ds(pl.multiple_of(pl.program_id(0) * 128, 128), 128)
    both = mm(halo[...], jnp.concatenate([wk_ref[...], wv_ref[...]], 1))
    hk = both[:, :128].astype(BF16)
    hv = (both[:, 128:] + shift_v[:, lanes]).astype(BF16)
    hk_ref[...] = hk
    hv_ref[...] = hv
    kx[own_rows(core), :] = k_ref[...]
    kx[halo_rows(core), :] = hk
    vx[own_rows(core), :] = v_ref[...]
    vx[halo_rows(core), :] = hv
    vt[...] = vx[...].T

    def place(i):
        key_at, own_at = tile_place(i, core)
        return (
            pl.ds(pl.multiple_of(key_at, 128), KEY_TILES[i] * 128),
            pl.ds(pl.multiple_of(own_at, 128), 128),
            pl.ds(pl.multiple_of(core * 512 + own_at, 128), 128),
        )

    def scores_of(i):
        keys, own, _ = place(i)
        return mm_nt(kx[keys, :], stack_heads(q_ref[own, :]))

    scores = scores_of(0)
    for i, tiles in enumerate(KEY_TILES):
        following = scores_of(i + 1) if i < 3 else None
        keys, own, whole = place(i)
        mask = bias[pl.ds(BIAS_AT[i], tiles * 128), :]
        scores = jnp.concatenate([scores[:, :128] + mask, scores[:, 128:] + mask], 1)
        top = jnp.max(scores, 0, keepdims=True)
        exps = jnp.exp(scores - top)
        total = jnp.sum(exps, 0, keepdims=True)
        valid = jnp.where(seg_ref[:, whole] >= 0, 1.0, 0.0).astype(F32)
        mixed = mm(vt[:, keys], exps.astype(BF16))
        inverse = 1.0 / total
        out = jnp.concatenate(
            [
                mixed[:HEAD_DIM, :128] * (inverse[:, :128] * valid),
                mixed[HEAD_DIM:, 128:] * (inverse[:, 128:] * valid),
            ],
            0,
        )
        out = out.astype(BF16)
        attt_ref[:, own] = out
        att_ref[own, :] = out.T
        logs = top + jnp.log(total)
        lse_ref[0, 0:1, own] = logs[:, :128]
        lse_ref[0, 1:2, own] = logs[:, 128:]
        scores = following


def attend_call(info, seg, halo_tok, gain, shift, w, bv, qkv):
    return call(
        attend_kernel,
        "attend",
        (6,),
        [
            once((1, 1024)),
            pl.BlockSpec((HALO, D), lambda p, info: (info[0], 0), pipeline_mode=pl.Buffered(1)),
            once((D,)),
            once((D,)),
            pl.BlockSpec((D, 128), lambda p, info: (0, 6 + p)),
            pl.BlockSpec((D, 128), lambda p, info: (0, 12 + p)),
            once((D,)),
            pl.BlockSpec((512, 128), lambda p, info: (0, p)),
            pl.BlockSpec((512, 128), lambda p, info: (0, 6 + p)),
            pl.BlockSpec((512, 128), lambda p, info: (0, 12 + p)),
        ],
        [
            pl.BlockSpec((512, 128), lambda p, info: (0, p)),
            pl.BlockSpec((128, 512), lambda p, info: (p, 0)),
            pl.BlockSpec((1, 2, 512), lambda p, info: (p, 0, 0)),
            pl.BlockSpec((HALO, 128), lambda p, info: (0, p)),
            pl.BlockSpec((HALO, 128), lambda p, info: (0, p)),
        ],
        [
            moves((512, D), BF16),
            moves((D, 512), BF16),
            moves((6, 2, 512), F32),
            stays((HALO, D), BF16),
            stays((HALO, D), BF16),
        ],
        (info, Stays(seg), halo_tok, Stays(gain), Stays(shift), Stays(w), Stays(w), Stays(bv), Stays(qkv), Stays(qkv), Stays(qkv)),
        [
            pltpu.VMEM((768, 128), F32),
            pltpu.VMEM((BIAS_ROWS, 128), F32),
            pltpu.VMEM((HALO, D), BF16),
            pltpu.VMEM((1, D), F32),
            pltpu.VMEM((768, 128), BF16),
            pltpu.VMEM((768, 128), BF16),
            pltpu.VMEM((128, 768), BF16),
        ],
    )


def attend_back_kernel(
    info, seg_ref, q_ref, k_ref, v_ref, hk_ref, hv_ref, do_ref, lse_ref, delta_ref,
    own_ref, halo_ref, segk, bias, kx, vx, kt, dk, dv
):
    core = info[0]

    @pl.when(pl.program_id(0) == 0)
    def _():
        build_bias(seg_ref, core, segk, bias)

    kx[own_rows(core), :] = k_ref[...]
    kx[halo_rows(core), :] = hk_ref[...]
    vx[own_rows(core), :] = v_ref[...]
    vx[halo_rows(core), :] = hv_ref[...]
    kt[...] = kx[...].T
    dk[...] = jnp.zeros_like(dk)
    dv[...] = jnp.zeros_like(dv)

    def products(i):
        key_at, own_at = tile_place(i, core)
        keys = pl.ds(pl.multiple_of(key_at, 128), KEY_TILES[i] * 128)
        own = pl.ds(pl.multiple_of(own_at, 128), 128)
        queries = stack_heads(q_ref[own, :])
        grads = stack_heads(do_ref[own, :])
        return keys, own, queries, grads, mm_nt(kx[keys, :], queries), mm_nt(vx[keys, :], grads)

    ready = products(0)
    for i, tiles in enumerate(KEY_TILES):
        following = products(i + 1) if i < 3 else None
        keys, own, queries, grads, scores, grad_probs = ready
        mask = bias[pl.ds(BIAS_AT[i], tiles * 128), :]
        logs = jnp.concatenate([lse_ref[0, 0:1, own], lse_ref[0, 1:2, own]], 1)
        delta = jnp.concatenate([delta_ref[0, 0:1, own], delta_ref[0, 1:2, own]], 1)
        scores = jnp.concatenate([scores[:, :128] + mask, scores[:, 128:] + mask], 1)
        probs = jnp.exp(scores - logs)
        grad_scores = (probs * (grad_probs - delta)).astype(BF16)
        dv[keys, :] += mm(probs.astype(BF16), grads)
        dk[keys, :] += mm(grad_scores, queries)
        dq = mm(kt[:, keys], grad_scores) * HEAD_DIM ** (-0.5)
        dq = jnp.concatenate([dq[:HEAD_DIM, :128], dq[HEAD_DIM:, 128:]], 0)
        own_ref[0, own, :] = dq.T.astype(BF16)
        ready = following
    own_ref[1] = dk[own_rows(core), :].astype(BF16)
    own_ref[2] = dv[own_rows(core), :].astype(BF16)
    halo_ref[0] = dk[halo_rows(core), :].astype(BF16)
    halo_ref[1] = dv[halo_rows(core), :].astype(BF16)


def attend_back_call(which, info, seg, qkv, hk, hv, grad, lse, delta, after):
    def at(p, info):
        return p + (3 * info[0] if which else 3 * (1 - info[0]))

    return call(
        attend_back_kernel,
        "attend_back",
        (3,),
        [
            once((1, 1024)),
            pl.BlockSpec((512, 128), lambda p, info: (0, at(p, info))),
            pl.BlockSpec((512, 128), lambda p, info: (0, 6 + at(p, info))),
            pl.BlockSpec((512, 128), lambda p, info: (0, 12 + at(p, info))),
            pl.BlockSpec((HALO, 128), lambda p, info: (0, at(p, info))),
            pl.BlockSpec((HALO, 128), lambda p, info: (0, at(p, info))),
            pl.BlockSpec((512, 128), lambda p, info: (0, at(p, info))),
            pl.BlockSpec((1, 2, 512), lambda p, info: (at(p, info), 0, 0)),
            pl.BlockSpec((1, 2, 512), lambda p, info: (at(p, info), 0, 0)),
        ],
        [
            pl.BlockSpec((3, 512, 128), lambda p, info: (0, 0, p)),
            pl.BlockSpec((2, HALO, 128), lambda p, info: (0, 0, p)),
        ],
        [
            moves((3, 512, 384), BF16),
            moves((2, HALO, 384), BF16),
        ],
        (info, Stays(seg), Stays(qkv), Stays(qkv), Stays(qkv), Stays(hk), Stays(hv), grad, lse, delta),
        [
            pltpu.VMEM((768, 128), F32),
            pltpu.VMEM((BIAS_ROWS, 128), F32),
            pltpu.VMEM((768, 128), BF16),
            pltpu.VMEM((768, 128), BF16),
            pltpu.VMEM((128, 768), BF16),
            pltpu.VMEM((768, 128), F32),
            pltpu.VMEM((768, 128), F32),
        ],
        after=after,
    )


def gelu_parts(value):
    size = jnp.abs(value)
    density = jnp.exp(-0.5 * value * value)
    t = 1.0 / (1.0 + 0.23164189 * size)
    poly = t * (0.127414796 + t * (-0.142248368 + t * (0.7107068705 + t * (-0.7265760135 + t * 0.5307027145))))
    tail = poly * density
    return jnp.where(value >= 0, 1.0 - tail, tail), density * 0.3989422804014327


def mlp_kernel(
    info, seg_ref, att_ref, wp_ref, bp_ref, gain_ref, shift_ref, b1_ref, b2_ref, tok_hbm, cot_hbm, w1_hbm, w2_hbm,
    out_ref, actt_ref, send_ref, keep_ref, normt_ref, gb_ref, do_ref, delta_ref, bias1_ref, sums_ref,
    low, middle, final, back, tok, cot, w1, w2, block, shift_one, valid, sems
):
    step = pl.program_id(0)
    core = info[0]

    def fetch(j):
        slot = j % 2
        lanes = pl.ds(pl.multiple_of(((j + 2 * (1 - core)) % 4) * 768, 768), 768)
        return (
            pltpu.make_async_copy(w1_hbm.at[:, lanes], w1.at[slot], sems.at[0, slot]),
            pltpu.make_async_copy(w2_hbm.at[lanes, :], w2.at[slot], sems.at[1, slot]),
        )

    tok_copy = pltpu.make_async_copy(tok_hbm, tok, sems.at[2, 1])
    cot_copy = pltpu.make_async_copy(cot_hbm, cot, sems.at[2, 0])

    @pl.when(step == 0)
    def _():
        tok_copy.start()
        begin(fetch(0))
        cot_copy.start()
        column_valid(seg_ref, core, valid)
        branch = mm(att_ref[...], wp_ref[...]) + row_of(bp_ref)
        tok_copy.wait()
        value = tok[...].astype(F32) + branch
        middle[...] = value
        final[...] = value + row_of(b2_ref)
        unit, _ = norm_unit(value)
        normed = (unit * row_of(gain_ref) + row_of(shift_ref)).astype(BF16)
        low[...] = normed
        normt_ref[...] = normed.T
        shift_one[...] = row_of(b1_ref)
        back[...] = jnp.zeros_like(back)
        cot_copy.wait()

    @pl.when((step > 0) & (step < 4))
    def _():
        begin(fetch(step))

    @pl.when(step > 0)
    def _():
        now = step - 1
        finish(fetch(now))
        slot = now % 2
        at_unit = ((now + 2 * (1 - core)) % 4) * 768
        shift = shift_one[:, pl.ds(pl.multiple_of(at_unit, 128), 768)]
        w1_now, w2_now = w1.at[slot], w2.at[slot]
        chunk = 256
        products = [
            (mm(low[at : at + chunk, :], w1_now[...]), mm_nt(cot[at : at + chunk, :], w2_now[...]))
            for at in range(0, 512, chunk)
        ]
        total = jnp.zeros((1, 768), F32)
        for at, (hidden, lifted) in zip(range(0, 512, chunk), products):
            rows = pl.ds(at, chunk)
            hidden = hidden + shift
            cdf, pdf = gelu_parts(hidden)
            active = (hidden * cdf).astype(BF16)
            grad = (lifted * (cdf + hidden * pdf)).astype(BF16)
            actt_ref[:, rows] = active.T
            block[rows, :] = grad
            total += jnp.sum(grad.astype(F32), 0, keepdims=True)
            final[rows, :] += mm(active, w2_now[...])
            back[rows, :] += mm_nt(grad, w1_now[...])
        bias1_ref[...] = total

        @pl.when(now < 2)
        def _():
            send_ref[...] = block[...]

        @pl.when(now >= 2)
        def _():
            keep_ref[...] = block[...]

    @pl.when(step == 4)
    def _():
        mask = valid[...]
        done = final[...]
        out_ref[0] = done.astype(BF16)
        for k in range(0, D, 128):
            part = done[:, k : k + 128]
            kept = part * mask
            sums_ref[4:5, k : k + 128] = jnp.sum(kept, 0, keepdims=True)
            sums_ref[5:6, k : k + 128] = jnp.sum(kept * part, 0, keepdims=True)
            sums_ref[6:7, k : k + 128] = jnp.sum(mask, 0, keepdims=True)
        sums_ref[7:8, :] = jnp.zeros((1, D), F32)
        grad = back[...]
        unit, inv_scale = norm_unit(middle[...])
        sums_ref[0:1, :] = jnp.sum(grad * unit, 0, keepdims=True)
        sums_ref[1:2, :] = jnp.sum(grad, 0, keepdims=True)
        wide = cot[...].astype(F32)
        branch = (wide + norm_back(grad, unit, inv_scale, row_of(gain_ref))).astype(BF16)
        gb_ref[...] = branch
        sums_ref[2:3, :] = jnp.sum(branch.astype(F32), 0, keepdims=True)
        sums_ref[3:4, :] = jnp.sum(wide, 0, keepdims=True)
        grad_att = mm_nt(branch, wp_ref[...]).astype(BF16).astype(F32)
        grad_att = jnp.concatenate([grad_att[:, k : k + 128] * mask for k in range(0, D, 128)], 1)
        do_ref[...] = grad_att.astype(BF16)
        prod = grad_att * att_ref[...].astype(F32)
        high = prod.astype(BF16)
        rest = (prod - high.astype(F32)).astype(BF16)
        pick = lax.broadcasted_iota(jnp.int32, (16, D), 1) // HEAD_DIM == lax.broadcasted_iota(jnp.int32, (16, D), 0)
        pick = jnp.where(pick, 1.0, 0.0).astype(BF16)
        delta = mm_nt(pick, high) + mm_nt(pick, rest)
        for pair in range(6):
            delta_ref[pair] = delta[2 * pair : 2 * pair + 2, :]


def mlp_call(info, seg, att, tok, cot, wp, bp, gain, shift, w1, b1, w2, b2, after):
    def quarter(j, info):
        return (jnp.maximum(j - 1, 0) + 2 * (1 - info[0])) % 4

    return call(
        mlp_kernel,
        "mlp",
        (5,),
        [
            once((1, 1024)),
            once((512, D)),
            once((D, D)),
            once((D,)),
            once((D,)),
            once((D,)),
            once((FF,)),
            once((D,)),
        ]
        + [pl.BlockSpec(memory_space=pl.ANY)] * 4,
        [
            full((1, 512, D)),
            pl.BlockSpec((768, 512), lambda j, info: (quarter(j, info), 0)),
            pl.BlockSpec((512, 768), lambda j, info: (0, jnp.clip(j - 1, 0, 1))),
            pl.BlockSpec((512, 768), lambda j, info: (0, jnp.maximum(j - 3, 0))),
            full((D, 512)),
            full((512, D)),
            full((512, D)),
            full((6, 2, 512)),
            pl.BlockSpec((1, 768), lambda j, info: (0, quarter(j, info))),
            full((8, D)),
        ],
        [
            stays((1, 512, D), BF16),
            moves((FF, 512), BF16),
            moves((512, FF // 2), BF16),
            moves((512, FF // 2), BF16),
            moves((D, 512), BF16),
            moves((512, D), BF16),
            moves((512, D), BF16),
            moves((6, 2, 512), F32),
            moves((1, FF), F32),
            moves((8, D), F32),
        ],
        (info, Stays(seg), att, Stays(wp), Stays(bp), Stays(gain), Stays(shift), Stays(b1), Stays(b2))
        + (Stays(tok), Stays(cot), Stays(w1), Stays(w2)),
        [
            pltpu.VMEM((512, D), BF16),
            pltpu.VMEM((512, D), F32),
            pltpu.VMEM((512, D), F32),
            pltpu.VMEM((512, D), F32),
            pltpu.VMEM((512, D), BF16),
            pltpu.VMEM((512, D), BF16),
            pltpu.VMEM((2, D, 768), BF16),
            pltpu.VMEM((2, 768, D), BF16),
            pltpu.VMEM((512, 768), BF16),
            pltpu.VMEM((1, FF), F32),
            pltpu.VMEM((512, 128), F32),
            pltpu.SemaphoreType.DMA((3, 2)),
        ],
        after=after,
    )


def input_kernel(
    info, one_ref, two_ref, halo_one_ref, halo_two_ref, w_ref, tok_ref, gb_ref, gain_ref,
    mlp_sums_ref, bias1_ref, gtok_ref, sums_ref, total, block, columns
):
    step = pl.program_id(0)
    core = info[0]
    near = pl.ds(pl.multiple_of((1 - core) * HALO, HALO), HALO)
    left, right = pl.ds(0, 384), pl.ds(384, 384)

    @pl.when(step == 0)
    def _():
        total[...] = jnp.zeros_like(total)

    block[:, left] = jnp.where(core == 0, two_ref[0], one_ref[0])
    block[:, right] = jnp.where(core == 0, one_ref[0], two_ref[0])

    @pl.when(step > 0)
    def _():
        low = jnp.where(core == 0, halo_two_ref[0], halo_one_ref[0])
        high = jnp.where(core == 0, halo_one_ref[0], halo_two_ref[0])
        block[near, left] = (block[near, left].astype(F32) + low.astype(F32)).astype(BF16)
        block[near, right] = (block[near, right].astype(F32) + high.astype(F32)).astype(BF16)

    grad = block[...]
    columns[step] = jnp.sum(grad.astype(F32), 0, keepdims=True)
    total[...] += mm_nt(grad, w_ref[...])

    @pl.when(step == 2)
    def _():
        grad = total[...]
        unit, inv_scale = norm_unit(tok_ref[...].astype(F32))
        sums_ref[0:1, :] = jnp.sum(grad * unit, 0, keepdims=True)
        sums_ref[1:2, :] = jnp.sum(grad, 0, keepdims=True)
        gtok_ref[0] = gb_ref[...].astype(F32) + norm_back(grad, unit, inv_scale, row_of(gain_ref))
        sums_ref[2:3, :] = columns[0]
        sums_ref[3:4, :] = columns[2]
        sums_ref[4:5, :] = mlp_sums_ref[2:3, :]
        sums_ref[5:7, :] = mlp_sums_ref[0:2, :]
        for k in range(4):
            sums_ref[7 + k : 8 + k, :] = bias1_ref[:, k * D : (k + 1) * D]
        sums_ref[11:12, :] = mlp_sums_ref[3:4, :]
        sums_ref[12:15, :] = mlp_sums_ref[4:7, :]
        sums_ref[15:16, :] = jnp.zeros((1, D), F32)


def input_call(info, one, two, halo_one, halo_two, w, tok, gb, gain, mlp_sums, bias1, after):
    return call(
        input_kernel,
        "input_grad",
        (3,),
        [
            pl.BlockSpec((1, 512, 384), lambda j, info: (j, 0, 0)),
            pl.BlockSpec((1, 512, 384), lambda j, info: (j, 0, 0)),
            pl.BlockSpec((1, HALO, 384), lambda j, info: (jnp.maximum(j - 1, 0), 0, 0)),
            pl.BlockSpec((1, HALO, 384), lambda j, info: (jnp.maximum(j - 1, 0), 0, 0)),
            pl.BlockSpec((D, D), lambda j, info: (0, j)),
            once((512, D)),
            once((512, D)),
            once((D,)),
            once((8, D)),
            once((1, FF)),
        ],
        [full((1, 512, D)), full((16, D))],
        [stays((1, 512, D), F32), moves((16, D), F32)],
        (info, one, two, halo_one, halo_two, Stays(w), Stays(tok), gb, Stays(gain), mlp_sums, bias1),
        [pltpu.VMEM((512, D), F32), pltpu.VMEM((512, D), BF16), pltpu.VMEM((3, 1, D), F32)],
        after=after,
    )


def piece_of(place, order):
    bits = len(order)
    return sum(((place >> (bits - 1 - k)) & 1) << bit for k, bit in enumerate(order))


def share_rows(info, place, rows, orders):
    mine = info[1]
    first, second = (piece_of(place, order) for order in orders)
    return pl.ds(pl.multiple_of((jnp.where(info[0] == 0, first, second) ^ mine) * rows, rows), rows)


def left_copies(info, left_own, left_other, both, sem, orders, rows, places):
    copies = []
    for k, place in enumerate(places):
        where = share_rows(info, place, rows, orders)
        into = pl.ds(k * rows, rows)
        copies.append(pltpu.make_async_copy(left_own.at[where, :], both.at[into, pl.ds(0, 512)], sem))
        copies.append(pltpu.make_async_copy(left_other.at[where, :], both.at[into, pl.ds(512, 512)], sem))
    return copies


def fc2_kernel(orders, info, own_ref, other_ref, grad_ref, grad_other_ref, keep_ref, send_ref, both, right, sems):
    rows = FF // 16
    step = pl.program_id(0)

    def copies(at, slot):
        places = [at * 4 + k for k in range(4)]
        return left_copies(info, own_ref, other_ref, both.at[slot], sems.at[slot], orders, rows, places)

    @pl.when(step == 0)
    def _():
        begin(copies(0, 0))
        right[0:512, :] = grad_ref[...]
        right[512:1024, :] = grad_other_ref[...]

    @pl.when(step < 3)
    def _():
        begin(copies(step + 1, (step + 1) % 2))

    finish(copies(step, step % 2))
    out = mm(both[step % 2], right[...]).astype(BF16)
    quarter = rows // 4
    out = jnp.concatenate(
        [
            jnp.concatenate([out[k * rows + q * quarter : k * rows + (q + 1) * quarter] for k in range(4)], 0)
            for q in range(4)
        ],
        1,
    )

    @pl.when(step < 2)
    def _():
        keep_ref[...] = out

    @pl.when(step >= 2)
    def _():
        send_ref[...] = out


def core_half(rows):
    return pl.BlockSpec((rows, 384), lambda j, info: (0, info[0]), pipeline_mode=pl.Buffered(1))


def fc2_call(orders, info, own, other, cot, cot_other, after):
    return call(
        functools.partial(fc2_kernel, orders),
        "fc2_grad",
        (4,),
        [
            pl.BlockSpec(memory_space=pl.ANY),
            pl.BlockSpec(memory_space=pl.ANY),
            core_half(512),
            core_half(512),
        ],
        [
            pl.BlockSpec((192, 1536), lambda j, info: (jnp.minimum(j, 1), 0)),
            pl.BlockSpec((192, 1536), lambda j, info: (jnp.maximum(j - 2, 0), 0)),
        ],
        [moves((384, 1536), BF16)] * 2,
        (info, own, other, Stays(cot), cot_other),
        [pltpu.VMEM((2, 768, 1024), BF16), pltpu.VMEM((1024, 384), BF16), pltpu.SemaphoreType.DMA((2,))],
        after=after,
    )


def fc1_kernel(
    orders, info, norm_own, norm_other, att_own, att_other, grad_ref, grad_other, gb_ref, gb_other,
    keep_ref, send_ref, both, both_att, right, sems
):
    step = pl.program_id(0)
    norm_copies = left_copies(info, norm_own, norm_other, both, sems.at[0], orders, 48, range(16))
    att_copies = left_copies(info, att_own, att_other, both_att, sems.at[1], orders, 48, range(16))

    @pl.when(step == 0)
    def _():
        begin(norm_copies)
        begin(att_copies)

    @pl.when(step < 2)
    def _():
        right[0:512, :] = grad_ref[...]
        right[512:1024, :] = grad_other[...]

    @pl.when(step == 0)
    def _():
        finish(norm_copies)

    @pl.when(step < 2)
    def _():
        out = mm(both[...], right[...]).astype(BF16)
        keep_ref[...] = out[0:384, :]
        send_ref[...] = out[384:768, :]

    @pl.when(step == 2)
    def _():
        right[0:512, 0:256] = grad_ref[:, 0:256]
        right[512:1024, 0:256] = grad_other[:, 0:256]
        right[0:512, 256:640] = gb_ref[...]
        right[512:1024, 256:640] = gb_other[...]
        finish(att_copies)
        out = mm(both[...], right[:, 0:256]).astype(BF16)
        keep_ref[:, 0:256] = out[0:384, :]
        send_ref[:, 0:256] = out[384:768, :]
        out = mm(both_att[...], right[:, 256:640]).astype(BF16)
        keep_ref[:, 256:640] = out[0:384, :]
        send_ref[:, 256:640] = out[384:768, :]


def fc1_call(orders, info, norm_own, norm_other, att_own, att_other, grad, grad_other, gb, gb_other, after):
    return call(
        functools.partial(fc1_kernel, orders),
        "fc1_grad",
        (3,),
        [pl.BlockSpec(memory_space=pl.ANY)] * 4
        + [pl.BlockSpec((512, 640), lambda j, info: (0, j))] * 2
        + [core_half(512), core_half(512)],
        [pl.BlockSpec((384, 640), lambda j, info: (0, j))] * 2,
        [moves((384, 1920), BF16)] * 2,
        (info, norm_own, norm_other, att_own, att_other, grad, grad_other, gb, gb_other),
        [
            pltpu.VMEM((D, 1024), BF16),
            pltpu.VMEM((D, 1024), BF16),
            pltpu.VMEM((1024, 640), BF16),
            pltpu.SemaphoreType.DMA((2,)),
        ],
        after=after,
    )


def qkv_grad_kernel(
    orders, info, norm_own, norm_other, own_ref, other_ref, halo_in_ref, halo_out_ref, keep_ref, send_ref, both, right, sem
):
    step = pl.program_id(0)
    core = info[0]
    copies = left_copies(info, norm_own, norm_other, both, sem.at[0], orders, 48, range(16))

    @pl.when(step == 0)
    def _():
        begin(copies)

    right[0:512, :] = own_ref[0]
    right[512:1024, :] = other_ref[0]

    @pl.when(step > 0)
    def _():
        near = pl.ds(pl.multiple_of((1 - core) * HALO, HALO), HALO)
        far = pl.ds(pl.multiple_of(512 + core * HALO, HALO), HALO)
        right[near, :] = (right[near, :].astype(F32) + halo_in_ref[0].astype(F32)).astype(BF16)
        right[far, :] = (right[far, :].astype(F32) + halo_out_ref[0].astype(F32)).astype(BF16)

    @pl.when(step == 0)
    def _():
        finish(copies)

    out = mm(both[...], right[...]).astype(BF16)
    keep_ref[...] = out[0:384, :]
    send_ref[...] = out[384:768, :]


def qkv_grad_call(orders, info, norm_own, norm_other, own, other, halo_in, halo_out, after):
    return call(
        functools.partial(qkv_grad_kernel, orders),
        "qkv_grad",
        (3,),
        [
            pl.BlockSpec(memory_space=pl.ANY),
            pl.BlockSpec(memory_space=pl.ANY),
            pl.BlockSpec((1, 512, 384), lambda j, info: (j, 0, 0)),
            pl.BlockSpec((1, 512, 384), lambda j, info: (j, 0, 0)),
            pl.BlockSpec((1, HALO, 384), lambda j, info: (jnp.maximum(j - 1, 0), 0, 0)),
            pl.BlockSpec((1, HALO, 384), lambda j, info: (jnp.maximum(j - 1, 0), 0, 0)),
        ],
        [pl.BlockSpec((384, 384), lambda j, info: (0, j))] * 2,
        [moves((384, 1152), BF16)] * 2,
        (info, norm_own, norm_other, own, other, halo_in, halo_out),
        [pltpu.VMEM((D, 1024), BF16), pltpu.VMEM((1024, 384), BF16), pltpu.SemaphoreType.DMA((1,))],
        after=after,
    )


def fold_kernel(info, keep_ref, got_ref, *outs):
    for k, out in enumerate(outs):
        out[...] = (keep_ref[k].astype(F32) + got_ref[k].astype(F32)).astype(BF16)


def fold(info, keep, got, parts, after=(), cost=None):
    rows, columns = keep.shape
    per = rows // parts
    grid = 2 if per % 96 == 0 else 1
    take = pl.BlockSpec((parts, per // grid, columns), lambda j, info: (0, j, 0))
    return call(
        fold_kernel,
        "fold",
        (grid,),
        [take, take],
        [pl.BlockSpec((per // grid, columns), lambda j, info: (j, 0))] * parts,
        [moves((per, columns), BF16)] * parts,
        (info, keep.reshape(parts, per, columns), got.reshape(parts, per, columns)),
        after=after,
        cost=cost,
    )


def total_kernel(info, *refs):
    pieces, out = refs[:-1], refs[-1]
    if len(pieces) == 4:
        left = pieces[0][...].astype(F32) + pieces[1][...].astype(F32)
        right = pieces[2][...].astype(F32) + pieces[3][...].astype(F32)
    else:
        left, right = pieces[0][...].astype(F32), pieces[1][...].astype(F32)
    out[...] = (left + right).astype(BF16)


def total(info, pieces, after=()):
    shape = pieces[1].shape
    return call(
        total_kernel,
        "total",
        (1,),
        [full(shape)] * len(pieces),
        full(shape),
        moves(shape, BF16),
        (info, *pieces),
        after=after,
    )


def add_kernel(info, left_ref, right_ref, out_ref):
    out_ref[...] = left_ref[...] + right_ref[...]


def add(info, left, right, after):
    shape = left.shape
    return call(
        add_kernel,
        "add",
        (1,),
        [full(shape)] * 2,
        full(shape),
        moves(shape, F32),
        (info, left, right),
        after=after,
    )


def join_kernel(groups, info, own_ref, other_ref, *outs):
    core = info[0]
    own, other = own_ref[...].astype(F32), other_ref[...].astype(F32)
    low, high = jnp.where(core == 0, own, other), jnp.where(core == 0, other, own)
    rows = own.shape[0]
    for (first, columns, parts, stacked), out in zip(groups, outs):
        per = columns // parts // 128
        for part in range(parts):
            for k in range(per):
                at = first + (part * per + k) * 128
                if stacked:
                    base, stride = part * rows * 2 * per + k, 2 * per
                else:
                    base, stride = part * 2 * per + k, 2 * per * parts
                out[pl.ds(base, rows, stride), :] = low[:, at : at + 128]
                out[pl.ds(base + per, rows, stride), :] = high[:, at : at + 128]


def join(info, own, other, groups, after):
    rows = own.shape[0]
    shapes = [(rows * group[1] * 2 // 128, 128) for group in groups]
    return call(
        functools.partial(join_kernel, groups),
        "join",
        (1,),
        [full(own.shape)] * 2,
        [full(shape) for shape in shapes],
        [stays(shape, F32) for shape in shapes],
        (info, own, other),
        after=after,
    )


def pairs(count, masks):
    return [(2 * row + core, 2 * (row ^ masks[core]) + core) for row in range(count) for core in range(2)]


AXES = ("rows", "seq")


def swap_cores(value):
    return lax.ppermute(value, "seq", ((0, 1), (1, 0)))


def exchange(value, count, orders, level):
    return lax.ppermute(value, AXES, pairs(count, [1 << order[level] for order in orders]))


def scatter_plain(keep, send, groups):
    whole = jnp.concatenate([keep, send], 0)
    outs = []
    for first, columns, parts, stacked in groups:
        part = whole[:, first : first + columns]
        if stacked:
            part = part.reshape(16, 48, parts, columns // parts).transpose(0, 2, 1, 3).reshape(768 * parts, -1)
        share = lax.psum_scatter(part, "rows", scatter_dimension=0, tiled=True)
        rows = share.shape[0]
        both = lax.all_gather(share, "seq", axis=0).astype(F32)
        cuts = 1 if stacked else parts
        both = both.reshape(2, rows, cuts, -1)
        outs.append(both.transpose(1, 2, 0, 3).reshape(-1, 128))
    return outs


def sum_all(value, count):
    value = value + swap_cores(value)
    for bit in range(count.bit_length() - 1):
        value = value + lax.ppermute(value, AXES, pairs(count, (1 << bit, 1 << bit)))
    return value


def results_kernel(info, sums_ref, *outs):
    rows = ((0, 1), (1, 1), (2, 1), (3, 1), (4, 1), (5, 1), (6, 1), (7, 4), (11, 1))
    for (row, count), out in zip(rows, outs):
        for k in range(count):
            out[pl.ds(k * D, D)] = sums_ref[row + k, :]
    kept = sums_ref[14:15, :]
    mean = sums_ref[12:13, :] / kept
    outs[9][...] = (sums_ref[13:14, :] / kept - mean * mean).reshape(D)


def results(info, sums, after):
    widths = [D] * 7 + [FF] + [D] * 2
    return call(
        results_kernel,
        "results",
        (1,),
        [full((16, D))],
        [full((width,)) for width in widths],
        [stays((width,), F32) for width in widths],
        (info, sums),
        after=after,
    )


def per_device(
    count,
    tokens,
    segment_ids,
    ln1_gain,
    ln1_bias,
    w_qkv,
    bias_q,
    bias_v,
    w_proj,
    bias_proj,
    ln2_gain,
    ln2_bias,
    w_fc1,
    bias_fc1,
    w_fc2,
    bias_fc2,
    cotangent,
):
    ladder = count == 16
    core = lax.axis_index("seq").astype(jnp.int32)
    mine = lax.axis_index("rows").astype(jnp.int32)
    info = jnp.stack([core, mine])
    if ladder:
        info_shares = info
        order_two = ((1, 2, 3, 0), (2, 0, 3, 1))
        order_one = ((0, 1, 2, 3), (1, 2, 0, 3))
        order_qkv = ((0, 1, 2, 3), (1, 0, 2, 3))
    else:
        info_shares = info * jnp.array([1, 0], jnp.int32)
        order_two = order_one = order_qkv = ((3, 2, 1, 0), (3, 2, 1, 0))
    tok = tokens[0]
    cot = cotangent[0]

    tok_other = swap_cores(tok)
    cot_other = swap_cores(cot)
    qkv, normt = qkv_call(info, tok, ln1_gain, ln1_bias, w_qkv, bias_q, bias_v)
    normt_other = swap_cores(normt)
    att, attt, lse, hk, hv = attend_call(info, segment_ids, tok_other, ln1_gain, ln1_bias, w_qkv, bias_v, qkv)
    attt_other = swap_cores(attt)
    output, actt, gh_send, gh, normt_two, gb, grad_att, delta, bias1, mlp_sums = mlp_call(
        info,
        segment_ids,
        att,
        tok,
        cot,
        w_proj,
        bias_proj,
        ln2_gain,
        ln2_bias,
        w_fc1,
        bias_fc1,
        w_fc2,
        bias_fc2,
        (normt_other, cot_other),
    )
    actt_other = swap_cores(actt)
    gh_other = swap_cores(gh_send)
    normt_two_other = swap_cores(normt_two)
    gb_other = swap_cores(gb)
    first, halo_first = attend_back_call(0, info, segment_ids, qkv, hk, hv, grad_att, lse, delta, ())
    first_other = swap_cores(first)
    halo_first_other = swap_cores(halo_first)
    keep_two, send_two = fc2_call(order_two, info_shares, actt, actt_other, cot, cot_other, (halo_first,))
    if ladder:
        got_two = exchange(send_two, count, order_two, 0)
    keep_one, send_one = fc1_call(
        order_one, info_shares, normt_two, normt_two_other, attt, attt_other, gh, gh_other, gb, gb_other, (keep_two,)
    )
    if ladder:
        got_one = exchange(send_one, count, order_one, 0)
    second, halo_second = attend_back_call(
        1, info, segment_ids, qkv, hk, hv, grad_att, lse, delta, (keep_one,)
    )
    halo_second_other = swap_cores(halo_second)
    keep_qkv, send_qkv = qkv_grad_call(
        order_qkv, info_shares, normt, normt_other, second, first_other, halo_first_other, halo_second, ()
    )
    after = (keep_qkv,)
    if ladder:
        got_qkv = exchange(send_qkv, count, order_qkv, 0)
        keep_two, send_two = fold(info, keep_two, got_two, 2, after)
        got_two = exchange(send_two, count, order_two, 1)
        after = (keep_two,)
    grad_tokens, sums = input_call(
        info,
        first,
        second,
        halo_second_other,
        halo_first_other,
        w_qkv,
        tok,
        gb,
        ln1_gain,
        mlp_sums,
        bias1,
        after,
    )
    groups_two = ((0, 1536, 4, True),)
    groups_one = ((0, 1536, 1, False), (1536, 384, 1, False))
    groups_qkv = ((0, 1152, 3, False),)
    if ladder:
        steps = [lambda value: swap_cores(value)] + [
            lambda value, bit=bit: lax.ppermute(value, AXES, pairs(count, (1 << bit, 1 << bit))) for bit in range(4)
        ]
        arrived = steps[0](sums)
        keep_one, send_one = fold(info, keep_one, got_one, 2, (sums,))
        got_one = exchange(send_one, count, order_one, 1)
        keep_two, send_two = fold(info, keep_two, got_two, 2, (keep_one,))
        got_two = exchange(send_two, count, order_two, 2)
        sums = add(info, sums, arrived, (keep_two,))
        arrived = steps[1](sums)
        keep_qkv, send_qkv = fold(info, keep_qkv, got_qkv, 2, (sums,))
        got_qkv = exchange(send_qkv, count, order_qkv, 1)
        sums = add(info, sums, arrived, (keep_qkv,))
        arrived = steps[2](sums)
        keep_two, send_two = fold(info, keep_two, got_two, 2, (sums,))
        got_two = exchange(send_two, count, order_two, 3)
        keep_one, send_one = fold(info, keep_one, got_one, 2, (keep_two,))
        got_one = exchange(send_one, count, order_one, 2)
        keep_qkv, send_qkv = fold(info, keep_qkv, got_qkv, 2, (keep_one,))
        got_qkv = exchange(send_qkv, count, order_qkv, 2)
        sums = add(info, sums, arrived, (keep_qkv,))
        arrived = steps[3](sums)
        keep_one, send_one = fold(info, keep_one, got_one, 2, (sums,))
        got_one = exchange(send_one, count, order_one, 3)
        keep_qkv, send_qkv = fold(info, keep_qkv, got_qkv, 2, (keep_one,))
        got_qkv = exchange(send_qkv, count, order_qkv, 3)
        share_two = total(info, (keep_two, got_two), (keep_qkv,))
        other_two = swap_cores(share_two)
        sums = add(info, sums, arrived, (share_two,))
        arrived = steps[4](sums)
        share_one = total(info, (keep_one, got_one), (sums,))
        other_one = swap_cores(share_one)
        (grad_fc2,) = join(info, share_two, other_two, groups_two, (share_one,))
        share_qkv = total(info, (keep_qkv, got_qkv), (Stays(grad_fc2),))
        other_qkv = swap_cores(share_qkv)
        grad_fc1, grad_proj = join(info, share_one, other_one, groups_one, (share_qkv,))
        sums = add(info, sums, arrived, (Stays(grad_proj),))
        small = results(info, sums, ())
        (grad_qkv,) = join(info, share_qkv, other_qkv, groups_qkv, (Stays(small[0]),))
    else:
        (grad_fc2,) = scatter_plain(keep_two, send_two, groups_two)
        grad_fc1, grad_proj = scatter_plain(keep_one, send_one, groups_one)
        (grad_qkv,) = scatter_plain(keep_qkv, send_qkv, groups_qkv)
        small = results(info, sum_all(sums, count), ())
    return (
        output,
        grad_tokens,
        small[0],
        small[1],
        grad_qkv.reshape(-1),
        small[2],
        small[3],
        grad_proj.reshape(-1),
        small[4],
        small[5],
        small[6],
        grad_fc1.reshape(-1),
        small[7],
        grad_fc2.reshape(-1),
        small[8],
        small[9],
    )


def solution(mesh):
    split, whole, shares = P("rows", "seq", None), P(), P("rows")
    in_specs = (split, P("rows", None)) + (whole,) * 13 + (split,)
    out_specs = (split, split, whole, whole, shares, whole, whole, shares) + (whole,) * 3 + (shares, whole, shares, whole, whole)
    return jax.shard_map(
        functools.partial(per_device, mesh.shape["rows"]),
        mesh=mesh,
        in_specs=in_specs,
        out_specs=out_specs,
        check_vma=False,
    )
```
